32 devices in a mesh: item: 8 (over z, x), day: 4 (over y, core).
Axes of the slice: x: 2, y: 2, z: 4, core: 2. Of those that a mesh axis runs over, the one named last changes fastest.
Arguments:
- user_factors: float32 [256, 512], P(('item', 'day')), may hold values from 0.005 to 0.012
- item_factors: bfloat16 [4096, 512], P('item'), may hold values from 0 to 1
- day_factors: bfloat16 [184, 512], P('day'), may hold values from 0.099609375 to 1
- tile_counts: bfloat16 [4096, 128, 128], P(('item', 'day')), may hold values from 0 to 2
- tile_index: int32 [3, 4096], P(None, ('item', 'day')), may hold values from 0 to 45, as said below
- tile_live: int32 [32], P(('item', 'day')), may hold values from 32 to 128, as said below
Outputs:
- updated_users: float32 [256, 512], P(('item', 'day'))
The draws below stay inside these ranges and needn't reach their ends.
Inputs may be any that keep to these rules, and one draw needn't show every extreme that they name: `tile_index`: row 0 names a user block below 2, row 1 an item block below 4 and row 2 a day below 46, local to the device that holds the slot. Only the first tile_live[d] slots of list d are live; some list has all 128 live.
All inputs are finite; a program needn't handle non-finite values.
Results may differ from the reference program's by a relative error of at most 0.003.
Values may be sent and summed in bfloat16 or wider, within the bound.
No kernel may reach another device: no remote copies, remote signals or barrier semaphores. Data moves between devices by JAX's collectives and lax.ppermute only.
A program may use at most 64 MiB of HBM per device.

```python
import math
import jax
import jax.numpy as jnp
from jax import lax

R = 512
TILE = 128
GROUP = 8
CAP = 128
ITEMBLK_DEV = 4
DAY_DEV = 46
USERS = 256
USER_BLOCKS = 2
ITEMS = 4096
DAYS = 184
DEVICE_SLOTS = 32
TILES_ALL = 4096
COUNT_SCALE = 2
N_ITEM = 8
N_DAY = 4


def draw_layout(key):
    first, second, third = jax.random.split(jax.random.fold_in(key, 11), 3)
    users = jax.random.randint(first, (TILES_ALL,), 0, USER_BLOCKS, dtype=jnp.int32)
    items = jax.random.randint(second, (TILES_ALL,), 0, ITEMBLK_DEV, dtype=jnp.int32)
    days = jax.random.randint(third, (TILES_ALL,), 0, DAY_DEV, dtype=jnp.int32)
    return jnp.stack([users, items, days], axis=0)


def log_even(key, shape, low, high):
    spread = jax.random.uniform(key, shape, jnp.float32, jnp.log(low), jnp.log(high))
    return jnp.exp(spread)


def sparse_rows(key, shape, base_low, base_high, big_low, big_high):
    first, second, third = jax.random.split(key, 3)
    base = log_even(first, shape, base_low, base_high)
    large = log_even(second, shape, big_low, big_high)
    chance = 8.0 / R
    picked = jax.random.bernoulli(third, chance, shape)
    return jnp.where(picked, large, base)


def draw_tile_index(key, part):
    return draw_layout(key)


def draw_tile_live(key, part):
    first, second = jax.random.split(jax.random.fold_in(key, 23), 2)
    counts = jax.random.randint(first, (DEVICE_SLOTS,), CAP // 4, CAP // 2 + 1, dtype=jnp.int32)
    fullest = jax.random.randint(second, (), 0, DEVICE_SLOTS, dtype=jnp.int32)
    return counts.at[fullest].set(CAP)


def draw_user_factors(key, part):
    inner = jax.random.fold_in(key, 31)
    values = log_even(inner, (USERS, R), 0.005, 0.012)
    return values


def draw_item_factors(key, part):
    return sparse_rows(jax.random.fold_in(key, 37), (ITEMS, R), 0.005, 0.015, 0.2, 1.0).astype(jnp.bfloat16)


def draw_tile_counts(key, part):
    layout = draw_layout(key)
    first, second, third = jax.random.split(jax.random.fold_in(key, 41), 3)
    user_level = log_even(first, (USERS,), 0.5, 2.0)
    item_level = log_even(second, (ITEMS,), 0.5, 2.0)
    noise = log_even(third, (TILES_ALL, TILE, TILE), 0.5, 2.0)
    slots = jnp.arange(TILES_ALL, dtype=jnp.int32)
    item_group = slots // CAP // N_DAY
    inside = jnp.arange(TILE, dtype=jnp.int32)
    user_ids = layout[0][:, None] * TILE + inside[None, :]
    item_ids = (item_group * ITEMBLK_DEV + layout[1])[:, None] * TILE + inside[None, :]
    levels = user_level[user_ids][:, :, None] * item_level[item_ids][:, None, :]
    counts = COUNT_SCALE * levels * noise / 8.0
    return counts.astype(jnp.bfloat16)


def block_scale(key, dims, cuts, least, largest):
    def one(dim, parts):
        draws = jax.random.uniform(jax.random.fold_in(jax.random.fold_in(key, 6), dim), (parts,), jnp.float32, least / len(cuts), largest / len(cuts))
        return jnp.repeat(jnp.exp(draws), dims[dim] // parts).reshape((-1,) + (1,) * (len(dims) - dim - 1))

    level = one(*cuts[0])
    for cut in cuts[1:]:
        level = level * one(*cut)
    return level


def setup_inputs(seed: int = 0) -> dict:
    key_of = jax.random.split(jax.random.key(seed), 7)
    user_factors = draw_user_factors(jax.random.fold_in(key_of[6], 71), 0)
    item_factors = draw_item_factors(jax.random.fold_in(key_of[6], 71), 0)
    day_factors = jnp.clip(jnp.exp(math.log(1.0) - 2.306499 * jax.random.uniform(key_of[2], (DAYS, R), jnp.float32) ** block_scale(key_of[2], (DAYS, R), ((0, 4),), -0.2, 0.2)), 0.099609375, 1.0).astype(jnp.bfloat16)
    tile_counts = draw_tile_counts(jax.random.fold_in(key_of[6], 71), 0)
    tile_index = draw_tile_index(jax.random.fold_in(key_of[6], 71), 0)
    tile_live = draw_tile_live(jax.random.fold_in(key_of[6], 71), 0)
    return {"user_factors": user_factors, "item_factors": item_factors, "day_factors": day_factors, "tile_counts": tile_counts, "tile_index": tile_index, "tile_live": tile_live}


def reference(user_factors, item_factors, day_factors, tile_counts, tile_index, tile_live):
    user_rows = user_factors.astype(jnp.bfloat16).reshape(USER_BLOCKS, TILE, R)
    item_blocks = item_factors.reshape(ITEMBLK_DEV * N_ITEM, TILE, R)
    slots = jnp.arange(TILES_ALL, dtype=jnp.int32)
    device = slots // CAP
    position = slots % CAP
    item_group = device // N_DAY
    day_group = device % N_DAY
    user_ids = tile_index[0]
    item_ids = item_group * ITEMBLK_DEV + tile_index[1]
    day_ids = day_group * DAY_DEV + tile_index[2]
    live = position < tile_live[device]
    turns = TILES_ALL // GROUP
    stacked = (tile_counts.reshape(turns, GROUP, TILE, TILE), user_ids.reshape(turns, GROUP),
               item_ids.reshape(turns, GROUP), day_ids.reshape(turns, GROUP), live.reshape(turns, GROUP))

    def turn(phi, pieces):
        counts, users, items, days, active = pieces
        scales = day_factors[days].astype(jnp.float32)[:, None, :]
        item_rows = item_blocks[items].astype(jnp.float32)
        scaled = (user_rows[users].astype(jnp.float32) * scales).astype(jnp.bfloat16)
        model = jnp.einsum("gur,gir->gui", scaled.astype(jnp.float32), item_rows)
        ratio = jnp.where(active[:, None, None], counts.astype(jnp.float32) / model, 0.0).astype(jnp.bfloat16)
        weighted = (item_rows * scales).astype(jnp.bfloat16)
        terms = jnp.einsum("gui,gir->gur", ratio.astype(jnp.float32), weighted.astype(jnp.float32))
        return phi.at[users].add(terms), None

    phi, _ = lax.scan(turn, jnp.zeros((USER_BLOCKS, TILE, R), jnp.float32), stacked)
    totals = jnp.sum(item_factors.astype(jnp.float32), axis=0) * jnp.sum(day_factors.astype(jnp.float32), axis=0)
    return user_factors * phi.reshape(USERS, R) / totals
```

```python
import jax
import jax.numpy as jnp
from jax import lax
from jax.experimental import pallas as pl
from jax.experimental.pallas import tpu as pltpu
from jax.sharding import PartitionSpec as P

TILE = 128
GROUP = 8
LANES = 128


def tiles_kernel(index, live, place, users, items, days, counts, out, order, filled, day_rows, weighted, phi):
    blocks, rank = users.shape[0] // TILE, users.shape[1]
    own_live = live[0]

    def clear(u, carry):
        filled[u] = 0
        return carry

    lax.fori_loop(0, blocks, clear, 0)

    def enlist(s, carry):
        u = index[0, s]
        at = filled[u]
        order[u, at] = s
        filled[u] = at + 1
        return carry

    lax.fori_loop(0, own_live, enlist, 0)
    day_rows[...] = days[...].astype(jnp.float32)

    def user_block(u, carry):
        start = pl.multiple_of(u * TILE, TILE)
        rows = users[pl.ds(start, TILE), :]
        listed = filled[u]
        phi[...] = jnp.zeros_like(phi)

        def group(g, carry):
            tiles = []
            for j in range(GROUP):
                at = g * GROUP + j
                s = order[u, jnp.minimum(at, listed - 1)]
                item = pl.multiple_of(index[1, s] * TILE, TILE)
                scale = day_rows[pl.ds(index[2, s], 1), :].astype(jnp.bfloat16)
                weighted[pl.ds(j * TILE, TILE), :] = items[pl.ds(item, TILE), :] * scale
                tiles.append(jnp.where(at < listed, counts[s].astype(jnp.float32), 0.0))
            model = lax.dot_general(
                rows, weighted[...], (((1,), (1,)), ((), ())), preferred_element_type=jnp.float32
            )
            ratio = (jnp.concatenate(tiles, axis=1) / model).astype(jnp.bfloat16)
            phi[...] += jnp.dot(ratio, weighted[...], preferred_element_type=jnp.float32)
            return carry

        lax.fori_loop(0, (listed + GROUP - 1) // GROUP, group, 0)
        owners = TILE // out.shape[1]
        out[pl.ds(u * owners, owners), :, 0:rank] = (
            phi[...].reshape(owners, out.shape[1], rank).astype(jnp.bfloat16)
        )
        return carry

    lax.fori_loop(0, blocks, user_block, 0)

    item_sum = jnp.sum(items[...].astype(jnp.float32), axis=0, keepdims=True)
    day_sum = jnp.sum(day_rows[...], axis=0, keepdims=True)
    row = lax.broadcasted_iota(jnp.int32, (8, LANES), 0)
    extra = jnp.zeros((8, LANES), jnp.float32)
    for q in range(rank // LANES):
        for first, total, mine in ((0, item_sum, place[1]), (2, day_sum, place[0])):
            part = jnp.where(mine == q, total[:, q * LANES : (q + 1) * LANES], 0.0)
            high = part.astype(jnp.bfloat16).astype(jnp.float32)
            extra = jnp.where(row == first, extra + high, extra)
            extra = jnp.where(row == first + 1, extra + (part - high), extra)
    out[:, :, rank:] = jnp.broadcast_to(
        extra.astype(jnp.bfloat16)[None], (out.shape[0], 8, LANES)
    )


def finish_kernel(n_item, n_day, received, user_factors, out):
    rank = user_factors.shape[1]
    phi = jnp.sum(received[:, :, 0:rank].astype(jnp.float32), axis=0)
    for q in range(rank // LANES):
        cols = slice(q * LANES, (q + 1) * LANES)
        item = received[q, :, rank:].astype(jnp.float32)
        for i in range(1, n_item):
            item = item + received[i * n_day + q, :, rank:].astype(jnp.float32)
        day = received[q * n_day, :, rank:].astype(jnp.float32)
        for k in range(1, n_day):
            day = day + received[q * n_day + k, :, rank:].astype(jnp.float32)
        totals = (item[0:1] + item[1:2]) * (day[2:3] + day[3:4])
        out[:, cols] = user_factors[:, cols] * phi[:, cols] / totals


def solution(mesh):
    n_item, n_day = mesh.shape["item"], mesh.shape["day"]
    axes = ("item", "day")

    def per_device(user_factors, item_factors, day_factors, tile_counts, tile_index, tile_live):
        own, rank = user_factors.shape
        devices = n_item * n_day
        blocks = own * devices // TILE
        cap = tile_counts.shape[0]
        spread = jnp.broadcast_to(user_factors.astype(jnp.bfloat16)[None], (devices, own, rank))
        gathered = lax.all_to_all(spread, axes, 0, 0, tiled=True).reshape(devices * own, rank)
        place = jnp.stack([lax.axis_index("item"), lax.axis_index("day")]).astype(jnp.int32)
        vmem = pl.BlockSpec(memory_space=pltpu.VMEM)
        smem = pl.BlockSpec(memory_space=pltpu.SMEM)
        partial = pl.pallas_call(
            tiles_kernel,
            out_shape=jax.ShapeDtypeStruct((devices, own, rank + LANES), jnp.bfloat16),
            in_specs=[smem, smem, smem, vmem, vmem, vmem, vmem],
            out_specs=vmem,
            scratch_shapes=[
                pltpu.SMEM((blocks, cap), jnp.int32),
                pltpu.SMEM((blocks,), jnp.int32),
                pltpu.VMEM(day_factors.shape, jnp.float32),
                pltpu.VMEM((GROUP * TILE, rank), jnp.bfloat16),
                pltpu.VMEM((TILE, rank), jnp.float32),
            ],
            compiler_params=pltpu.CompilerParams(vmem_limit_bytes=40 * 1024 * 1024),
        )(tile_index, tile_live, place, gathered, item_factors, day_factors, tile_counts)
        received = lax.all_to_all(partial, axes, 0, 0, tiled=True)
        return pl.pallas_call(
            lambda *refs: finish_kernel(n_item, n_day, *refs),
            out_shape=jax.ShapeDtypeStruct((own, rank), jnp.float32),
            in_specs=[vmem, vmem],
            out_specs=vmem,
        )(received, user_factors)

    in_specs = (
        P(axes, None),
        P("item", None),
        P("day", None),
        P(axes, None, None),
        P(None, axes),
        P(axes),
    )
    return jax.shard_map(
        per_device, mesh=mesh, in_specs=in_specs, out_specs=P(axes, None), check_vma=False
    )
```

```python
import jax
import jax.numpy as jnp
from jax import lax
from jax.experimental import pallas as pl
from jax.experimental.pallas import tpu as pltpu
from jax.sharding import PartitionSpec as P

TILE = 128
GROUP = 4
UNROLL = 4
CHUNK = 16
LANES = 128
NEEDS = 8
VMEM = pl.BlockSpec(memory_space=pltpu.VMEM)
SMEM = pl.BlockSpec(memory_space=pltpu.SMEM)
HBM = pl.BlockSpec(memory_space=pltpu.HBM)
MIB = 1024 * 1024


def round_up(n, m):
    return (n + m - 1) // m * m


def plan_kernel(
    index_far, live_far, days_far, mate_index_far, mate_live_far, mate_days_far, items_far,
    plan, items, day_rows, extra,
    index, live, days, mate_index, mate_live, mate_days, spots, sems,
):
    rank = items.shape[1]
    fetch = [
        pltpu.make_async_copy(far, near, sems.at[i])
        for i, (far, near) in enumerate(
            (
                (index_far, index),
                (live_far, live),
                (mate_index_far, mate_index),
                (mate_live_far, mate_live),
                (days_far, days),
                (mate_days_far, mate_days),
                (items_far, items),
            )
        )
    ]
    for copy in fetch:
        copy.start()

    def clear(i, carry):
        for j in range(LANES):
            plan[i, j] = -1
        return carry

    lax.fori_loop(1, plan.shape[0], clear, 0)
    for j in range(LANES):
        plan[0, j] = 0
    for u in range(spots.shape[0]):
        spots[u] = 0
    for copy in fetch[:4]:
        copy.wait()

    mine, other = live[0], mate_live[0]
    half = (mine + other + 1) >> 1
    keep, mate_keep = jnp.minimum(mine, half), jnp.minimum(other, half)
    parts = jnp.maximum((keep + CHUNK - 1) // CHUNK, 2)
    mate_first = mate_keep // CHUNK
    mate_parts = jnp.where(mate_keep < other, (other + CHUNK - 1) // CHUNK - mate_first, 0)
    plan[0, 1] = parts
    plan[0, 2] = mate_first
    plan[0, 3] = parts + mate_parts

    def enlist(table, low, high, shift, day_shift, used):
        def place(u, code, tile, used):
            spot = spots[u]
            new = (spot & (GROUP - 1)) == 0
            spot = jnp.where(new, used * GROUP, spot)
            spots[u] = spot + 1
            plan[1 + (spot >> 7), spot & (LANES - 1)] = code
            plan[0, NEEDS + spot // (GROUP * UNROLL)] = (tile >> 4) + 1
            return used + new.astype(jnp.int32)

        def read(s):
            u, tile = table[0, s], s + shift
            code = (u << 24) | (tile << 16) | (table[1, s] << 8) | (table[2, s] + day_shift)
            return u, code, tile

        def four(t, used):
            found = [read(low + t * 4 + j) for j in range(4)]
            for u, code, tile in found:
                used = place(u, code, tile, used)
            return used

        def one(s, used):
            return place(*read(s), used)

        fours = (high - low) >> 2
        used = lax.fori_loop(0, fours, four, used)
        return lax.fori_loop(low + fours * 4, high, one, used)

    used = enlist(index, 0, keep, 0, 0, jnp.int32(0))
    used = enlist(
        mate_index, mate_keep, other, (parts - mate_first) * CHUNK, day_rows.shape[0] // 2, used
    )
    plan[0, 0] = (used + UNROLL - 1) // UNROLL

    for copy in fetch[4:]:
        copy.wait()
    count = days.shape[0]
    day_rows[0:count, :] = days[...].astype(jnp.float32)
    day_rows[day_rows.shape[0] // 2 : day_rows.shape[0] // 2 + count, :] = mate_days[...].astype(
        jnp.float32
    )
    day_sum = jnp.sum(days[...].astype(jnp.float32), axis=0, keepdims=True)
    item_sum = jnp.sum(items[...].astype(jnp.float32), axis=0, keepdims=True)
    item_at, day_at = lax.axis_index("item"), lax.axis_index("day")
    row = lax.broadcasted_iota(jnp.int32, (8, LANES), 0)
    block = jnp.zeros((8, LANES), jnp.float32)
    for q in range(rank // LANES):
        for first, total, at in ((0, item_sum, day_at), (2, day_sum, item_at)):
            part = jnp.where(at == q, total[:, q * LANES : (q + 1) * LANES], 0.0)
            high = part.astype(jnp.bfloat16).astype(jnp.float32)
            block = jnp.where(row == first, block + high, block)
            block = jnp.where(row == first + 1, block + (part - high), block)
    extra[...] = block


def tiles_kernel(
    plan_far, counts_far, mate_counts_far, users, items, day_rows, extra,
    out,
    plan, counts, phi, plan_sem, counts_sem, *buffers,
):
    weighted, ratios = buffers[:UNROLL], buffers[UNROLL:]
    rank = users.shape[1]
    fetch = pltpu.make_async_copy(plan_far, plan, plan_sem)
    fetch.start()

    def part(far, c, at):
        source = far.at[pl.ds(pl.multiple_of(c * CHUNK, CHUNK), CHUNK)]
        target = counts.at[pl.ds(pl.multiple_of(at * CHUNK, CHUNK), CHUNK)]
        return pltpu.make_async_copy(source, target, counts_sem.at[at])

    part(counts_far, 0, 0).start()
    part(counts_far, 1, 1).start()
    phi[...] = jnp.zeros_like(phi)
    weighted[-1][...] = jnp.zeros_like(weighted[-1])
    ratios[-1][...] = jnp.zeros_like(ratios[-1])
    fetch.wait()
    turns, parts, mate_first, all_parts = plan[0, 0], plan[0, 1], plan[0, 2], plan[0, 3]

    def start_part(c, carry):
        part(counts_far, c, c).start()
        return carry

    def start_mate_part(c, carry):
        part(mate_counts_far, mate_first + c - parts, c).start()
        return carry

    def wait_part(c, carry):
        part(counts_far, 0, c).wait()
        return carry

    lax.fori_loop(2, parts, start_part, 0)
    lax.fori_loop(parts, all_parts, start_mate_part, 0)
    out[:, :, rank:] = jnp.broadcast_to(
        extra[...].astype(jnp.bfloat16)[None], (out.shape[0], 8, LANES)
    )

    def code_at(spot):
        return plan[1 + (spot >> 7), spot & (LANES - 1)]

    def block_of(g):
        return pl.ds(pl.multiple_of((jnp.maximum(code_at(g * GROUP), 0) >> 24) * TILE, TILE), TILE)

    def make_ratio(g, i):
        rows = users[block_of(g), :]
        codes = [code_at(g * GROUP + j) for j in range(GROUP)]
        slots = [jnp.maximum(code, 0) for code in codes]
        for j, slot in enumerate(slots):
            item = pl.multiple_of(((slot >> 8) & 255) * TILE, TILE)
            scale = day_rows[pl.ds(slot & 255, 1), :].astype(jnp.bfloat16)
            weighted[i][j * TILE : (j + 1) * TILE, :] = items[pl.ds(item, TILE), :] * scale
        model = lax.dot_general(
            rows, weighted[i][...], (((1,), (1,)), ((), ())), preferred_element_type=jnp.float32
        )
        for j, slot in enumerate(slots):
            cols = slice(j * TILE, (j + 1) * TILE)
            ratio = counts[(slot >> 16) & 255].astype(jnp.float32) / model[:, cols]
            ratios[i][:, cols] = jnp.where(codes[j] >= 0, ratio, 0.0).astype(jnp.bfloat16)

    def add_terms(g, i):
        phi[block_of(g), :] += jnp.dot(
            ratios[i][...], weighted[i][...], preferred_element_type=jnp.float32
        )

    def turn(t, ready):
        need = jnp.maximum(plan[0, NEEDS + t], ready)
        lax.fori_loop(ready, need, wait_part, 0)
        for i in range(UNROLL):
            g = t * UNROLL + i
            make_ratio(g, i)
            add_terms(jnp.maximum(g - 1, 0), (i - 1) % UNROLL)
        return need

    ready = lax.fori_loop(0, turns, turn, jnp.int32(0))
    lax.fori_loop(ready, all_parts, wait_part, 0)
    add_terms(jnp.maximum(turns * UNROLL - 1, 0), UNROLL - 1)
    out[:, :, 0:rank] = phi[...].reshape(out.shape[0], out.shape[1], rank).astype(jnp.bfloat16)


def finish_kernel(n_item, n_day, received, user_factors, out):
    rank = user_factors.shape[1]
    phi = jnp.sum(received[:, :, 0:rank].astype(jnp.float32), axis=0)
    for q in range(rank // LANES):
        cols = slice(q * LANES, (q + 1) * LANES)
        item = received[q, :, rank:].astype(jnp.float32)
        for i in range(1, n_item):
            item = item + received[i * n_day + q, :, rank:].astype(jnp.float32)
        day = received[q * n_day, :, rank:].astype(jnp.float32)
        for k in range(1, n_day):
            day = day + received[q * n_day + k, :, rank:].astype(jnp.float32)
        totals = (item[0:1] + item[1:2]) * (day[2:3] + day[3:4])
        out[:, cols] = user_factors[:, cols] * phi[:, cols] / totals


def solution(mesh):
    n_item, n_day = mesh.shape["item"], mesh.shape["day"]
    devices = n_item * n_day
    axes = ("item", "day")
    mates = [(k, k ^ 1) for k in range(n_day)]

    def per_device(user_factors, item_factors, day_factors, tile_counts, tile_index, tile_live):
        own, rank = user_factors.shape
        blocks = own * devices // TILE
        cap = tile_counts.shape[0]
        day_space = round_up(day_factors.shape[0], 8)
        groups = round_up(cap // GROUP + blocks, UNROLL)
        plan_shape = (1 + pl.cdiv(groups * GROUP, LANES), LANES)
        mate_counts, mate_index, mate_live, mate_days = (
            lax.ppermute(x, "day", mates)
            for x in (tile_counts, tile_index, tile_live, day_factors)
        )
        spread = jnp.broadcast_to(user_factors.astype(jnp.bfloat16)[None], (devices, own, rank))
        gathered = lax.all_to_all(spread, axes, 0, 0, tiled=True).reshape(devices * own, rank)
        plan, items, day_rows, extra = pl.pallas_call(
            plan_kernel,
            out_shape=(
                jax.ShapeDtypeStruct(plan_shape, jnp.int32),
                jax.ShapeDtypeStruct(item_factors.shape, jnp.bfloat16),
                jax.ShapeDtypeStruct((2 * day_space, rank), jnp.float32),
                jax.ShapeDtypeStruct((8, LANES), jnp.float32),
            ),
            in_specs=[HBM] * 7,
            out_specs=(SMEM, VMEM, VMEM, VMEM),
            scratch_shapes=[
                pltpu.SMEM(tile_index.shape, jnp.int32),
                pltpu.SMEM(tile_live.shape, jnp.int32),
                pltpu.VMEM(day_factors.shape, jnp.bfloat16),
                pltpu.SMEM(tile_index.shape, jnp.int32),
                pltpu.SMEM(tile_live.shape, jnp.int32),
                pltpu.VMEM(day_factors.shape, jnp.bfloat16),
                pltpu.SMEM((blocks,), jnp.int32),
                pltpu.SemaphoreType.DMA((7,)),
            ],
            compiler_params=pltpu.CompilerParams(vmem_limit_bytes=16 * MIB),
        )(tile_index, tile_live, day_factors, mate_index, mate_live, mate_days, item_factors)
        partial = pl.pallas_call(
            tiles_kernel,
            out_shape=jax.ShapeDtypeStruct((devices, own, rank + LANES), jnp.bfloat16),
            in_specs=[HBM, HBM, HBM, VMEM, VMEM, VMEM, VMEM],
            out_specs=VMEM,
            scratch_shapes=[
                pltpu.SMEM(plan_shape, jnp.int32),
                pltpu.VMEM((cap + 2 * CHUNK, *tile_counts.shape[1:]), jnp.bfloat16),
                pltpu.VMEM((blocks * TILE, rank), jnp.float32),
                pltpu.SemaphoreType.DMA,
                pltpu.SemaphoreType.DMA((cap // CHUNK + 2,)),
            ]
            + [pltpu.VMEM((GROUP * TILE, rank), jnp.bfloat16)] * UNROLL
            + [pltpu.VMEM((TILE, GROUP * TILE), jnp.bfloat16)] * UNROLL,
            compiler_params=pltpu.CompilerParams(vmem_limit_bytes=51 * MIB),
        )(plan, tile_counts, mate_counts, gathered, items, day_rows, extra)
        received = lax.all_to_all(partial, axes, 0, 0, tiled=True)
        return pl.pallas_call(
            lambda *refs: finish_kernel(n_item, n_day, *refs),
            out_shape=jax.ShapeDtypeStruct((own, rank), jnp.float32),
            in_specs=[VMEM, VMEM],
            out_specs=VMEM,
            compiler_params=pltpu.CompilerParams(vmem_limit_bytes=16 * MIB),
        )(received, user_factors)

    in_specs = (
        P(axes, None),
        P("item", None),
        P("day", None),
        P(axes, None, None),
        P(None, axes),
        P(axes),
    )
    return jax.shard_map(
        per_device, mesh=mesh, in_specs=in_specs, out_specs=P(axes, None), check_vma=False
    )
```

```python
import functools

import jax
import jax.numpy as jnp
from jax import lax
from jax.experimental import pallas as pl
from jax.experimental.pallas import tpu as pltpu
from jax.sharding import PartitionSpec as P

TILE = 128
GROUP = 4
UNROLL = 4
CHUNK = 16
LANES = 128
NEEDS = 8
DAY_ROW = 4
FIRST = 2
PLAN_MIB = 50
VMEM = pl.BlockSpec(memory_space=pltpu.VMEM)
SMEM = pl.BlockSpec(memory_space=pltpu.SMEM)
ANY = pl.BlockSpec(memory_space=pl.ANY)
HBM = pl.BlockSpec(memory_space=pltpu.HBM)
MIB = 1024 * 1024


def round_up(n, m):
    return (n + m - 1) // m * m


def plan_kernel(
    index_far, live_far, days_far, mate_index_far, mate_live_far, mate_days_far, items_far, counts_far,
    plan, items, day_rows, first_counts,
    index, live, days, mate_index, mate_live, mate_days, spots, sems,
):
    fetch = [
        pltpu.make_async_copy(far, near, sems.at[i])
        for i, (far, near) in enumerate(
            (
                (index_far, index),
                (live_far, live),
                (mate_index_far, mate_index),
                (mate_live_far, mate_live),
                (days_far, days),
                (mate_days_far, mate_days),
                (items_far, items),
                (counts_far.at[pl.ds(0, first_counts.shape[0])], first_counts),
            )
        )
    ]
    for copy in fetch:
        copy.start()

    def clear(i, carry):
        for j in range(LANES):
            plan[i, j] = -1
        return carry

    lax.fori_loop(1, plan.shape[0], clear, 0)
    for j in range(LANES):
        plan[0, j] = 0
    for u in range(spots.shape[0]):
        spots[u] = 0
    for copy in fetch[:4]:
        copy.wait()

    mine, other = live[0], mate_live[0]
    half = (mine + other + 1) >> 1
    keep, mate_keep = jnp.minimum(mine, half), jnp.minimum(other, half)
    parts = jnp.maximum((keep + CHUNK - 1) // CHUNK, FIRST)
    mate_first = mate_keep // CHUNK
    mate_parts = jnp.where(mate_keep < other, (other + CHUNK - 1) // CHUNK - mate_first, 0)
    plan[0, 1] = parts
    plan[0, 2] = mate_first
    plan[0, 3] = parts + mate_parts

    def enlist(table, low, high, shift, day_shift, used):
        def place(u, code, tile, used):
            spot = spots[u]
            new = (spot & (GROUP - 1)) == 0
            spot = jnp.where(new, used * GROUP, spot)
            spots[u] = spot + 1
            plan[1 + (spot >> 7), spot & (LANES - 1)] = code
            plan[0, NEEDS + spot // (GROUP * UNROLL)] = (tile >> 4) + 1
            return used + new.astype(jnp.int32)

        def read(s):
            u, tile = table[0, s], s + shift
            code = (u << 24) | (tile << 16) | (table[1, s] << 8) | (table[2, s] + day_shift)
            return u, code, tile

        def four(t, used):
            found = [read(low + t * 4 + j) for j in range(4)]
            for u, code, tile in found:
                used = place(u, code, tile, used)
            return used

        def one(s, used):
            return place(*read(s), used)

        fours = (high - low) >> 2
        used = lax.fori_loop(0, fours, four, used)
        return lax.fori_loop(low + fours * 4, high, one, used)

    used = enlist(index, 0, keep, 0, 0, jnp.int32(0))
    used = enlist(
        mate_index, mate_keep, other, (parts - mate_first) * CHUNK, day_rows.shape[0] // 2, used
    )
    plan[0, 0] = used

    for copy in fetch[4:]:
        copy.wait()
    day_rows[...] = jnp.zeros_like(day_rows)
    count = days.shape[0]
    day_rows[0:count, :] = days[...].astype(jnp.float32)
    day_rows[day_rows.shape[0] // 2 : day_rows.shape[0] // 2 + count, :] = mate_days[...].astype(
        jnp.float32
    )


def sums_kernel(chips, kept, items, day_rows, extra):
    rank = items.shape[1]
    day_sum = jnp.sum(day_rows[...], axis=0, keepdims=True)
    item_sum = jnp.sum(items[...].astype(jnp.float32), axis=0, keepdims=True)
    item_at, chip_at = lax.axis_index("item"), lax.axis_index("day") >> 1
    row = lax.broadcasted_iota(jnp.int32, (8, LANES), 0)
    block = jnp.zeros((8, LANES), jnp.float32)
    for q in range(rank // LANES):
        for first, total, here in (
            (2 * (q // chips), item_sum, chip_at == q % chips),
            (DAY_ROW, day_sum, item_at == q),
        ):
            part = jnp.where(here, total[:, q * LANES : (q + 1) * LANES], 0.0)
            high = part.astype(jnp.bfloat16).astype(jnp.float32)
            block = jnp.where(row == first, block + high, block)
            block = jnp.where(row == first + 1, block + (part - high), block)
    extra[...] = block.astype(jnp.bfloat16)


def tiles_kernel(
    plan_far, counts_far, mate_counts_far, first_counts, users, items, day_rows,
    kept, sent,
    plan, counts, phi, plan_sem, counts_sem, *buffers,
):
    weighted, ratios = buffers[:UNROLL], buffers[UNROLL:]
    fetch = pltpu.make_async_copy(plan_far, plan, plan_sem)
    fetch.start()

    def part(far, c, at):
        source = far.at[pl.ds(pl.multiple_of(c * CHUNK, CHUNK), CHUNK)]
        target = counts.at[pl.ds(pl.multiple_of(at * CHUNK, CHUNK), CHUNK)]
        return pltpu.make_async_copy(source, target, counts_sem.at[at])

    counts[0 : FIRST * CHUNK] = first_counts[...]
    phi[...] = jnp.zeros_like(phi)
    weighted[-1][...] = jnp.zeros_like(weighted[-1])
    ratios[-1][...] = jnp.zeros_like(ratios[-1])
    fetch.wait()
    groups, parts, mate_first, all_parts = plan[0, 0], plan[0, 1], plan[0, 2], plan[0, 3]

    def start_part(c, carry):
        part(counts_far, c, c).start()
        return carry

    def start_mate_part(c, carry):
        part(mate_counts_far, mate_first + c - parts, c).start()
        return carry

    def wait_part(c, carry):
        part(counts_far, 0, c).wait()
        return carry

    lax.fori_loop(FIRST, parts, start_part, 0)
    lax.fori_loop(parts, all_parts, start_mate_part, 0)

    def code_at(spot):
        return plan[1 + (spot >> 7), spot & (LANES - 1)]

    def block_of(g):
        return pl.ds(pl.multiple_of((jnp.maximum(code_at(g * GROUP), 0) >> 24) * TILE, TILE), TILE)

    def make_ratio(g, i):
        rows = users[block_of(g), :]
        codes = [code_at(g * GROUP + j) for j in range(GROUP)]
        slots = [jnp.maximum(code, 0) for code in codes]
        for j, slot in enumerate(slots):
            item = pl.multiple_of(((slot >> 8) & 255) * TILE, TILE)
            scale = day_rows[pl.ds(slot & 255, 1), :].astype(jnp.bfloat16)
            weighted[i][j * TILE : (j + 1) * TILE, :] = items[pl.ds(item, TILE), :] * scale
        model = lax.dot_general(
            rows, weighted[i][...], (((1,), (1,)), ((), ())), preferred_element_type=jnp.float32
        )
        for j, slot in enumerate(slots):
            cols = slice(j * TILE, (j + 1) * TILE)
            ratio = counts[(slot >> 16) & 255].astype(jnp.float32) / model[:, cols]
            ratios[i][:, cols] = jnp.where(codes[j] >= 0, ratio, 0.0).astype(jnp.bfloat16)

    def add_terms(g, i):
        phi[block_of(g), :] += jnp.dot(
            ratios[i][...], weighted[i][...], preferred_element_type=jnp.float32
        )

    def turn(t, ready):
        need = jnp.maximum(plan[0, NEEDS + t], ready)
        lax.fori_loop(ready, need, wait_part, 0)
        for i in range(UNROLL):
            g = t * UNROLL + i
            make_ratio(g, i)
            add_terms(jnp.maximum(g - 1, 0), (i - 1) % UNROLL)
        return need

    rest = groups & (UNROLL - 1)
    turns = (groups >> 2) + (rest == UNROLL - 1).astype(jnp.int32)
    ready = lax.fori_loop(0, turns, turn, jnp.int32(FIRST))
    lax.fori_loop(ready, all_parts, wait_part, 0)
    g = turns * UNROLL

    @pl.when((rest == 1) | (rest == 2))
    def _():
        make_ratio(g, 0)
        add_terms(jnp.maximum(g - 1, 0), UNROLL - 1)
        add_terms(g, 0)

    @pl.when((rest != 1) & (rest != 2))
    def _():
        add_terms(jnp.maximum(g - 1, 0), UNROLL - 1)

    @pl.when(rest == 2)
    def _():
        make_ratio(g + 1, 1)
        add_terms(g + 1, 1)

    own = kept.shape[1]
    core = lax.axis_index("day") & 1
    for j in range(kept.shape[0]):
        kept[j] = phi[pl.ds(pl.multiple_of((2 * j + core) * own, own), own), :]
        sent[j] = phi[pl.ds(pl.multiple_of((2 * j + 1 - core) * own, own), own), :]


def finish_kernel(n_item, chips, received, user_factors, out):
    rank = user_factors.shape[1]
    phi = jnp.sum(received[:, :, 0:rank].astype(jnp.float32), axis=0)
    for q in range(rank // LANES):
        cols = slice(q * LANES, (q + 1) * LANES)
        item = received[q % chips, :, rank:].astype(jnp.float32)
        for i in range(1, n_item):
            item = item + received[i * chips + q % chips, :, rank:].astype(jnp.float32)
        day = received[q * chips, :, rank:].astype(jnp.float32)
        for k in range(1, chips):
            day = day + received[q * chips + k, :, rank:].astype(jnp.float32)
        at = 2 * (q // chips)
        totals = (item[at : at + 1] + item[at + 1 : at + 2]) * (
            day[DAY_ROW : DAY_ROW + 1] + day[DAY_ROW + 1 : DAY_ROW + 2]
        )
        out[:, cols] = user_factors[:, cols] * phi[:, cols] / totals


def solution(mesh):
    n_item, n_day = mesh.shape["item"], mesh.shape["day"]
    devices = n_item * n_day
    axes = ("item", "day")
    mates = [(k, k ^ 1) for k in range(n_day)]

    def per_device(user_factors, item_factors, day_factors, tile_counts, tile_index, tile_live):
        own, rank = user_factors.shape
        blocks = own * devices // TILE
        cap = tile_counts.shape[0]
        day_space = round_up(day_factors.shape[0], 8)
        groups = round_up(cap // GROUP + blocks, UNROLL)
        plan_shape = (1 + pl.cdiv(groups * GROUP, LANES), LANES)
        mate_counts, mate_index, mate_live, mate_days = (
            lax.ppermute(x, "day", mates)
            for x in (tile_counts, tile_index, tile_live, day_factors)
        )
        spread = jnp.broadcast_to(user_factors.astype(jnp.bfloat16)[None], (devices, own, rank))
        gathered = lax.all_to_all(spread, axes, 0, 0, tiled=True).reshape(devices * own, rank)
        plan, items, day_rows, first_counts = pl.pallas_call(
            plan_kernel,
            out_shape=(
                jax.ShapeDtypeStruct(plan_shape, jnp.int32),
                jax.ShapeDtypeStruct(item_factors.shape, jnp.bfloat16),
                jax.ShapeDtypeStruct((2 * day_space, rank), jnp.float32),
                jax.ShapeDtypeStruct((FIRST * CHUNK, *tile_counts.shape[1:]), jnp.bfloat16),
            ),
            in_specs=[HBM] * 8,
            out_specs=(SMEM, VMEM, VMEM, VMEM),
            scratch_shapes=[
                pltpu.SMEM(tile_index.shape, jnp.int32),
                pltpu.SMEM(tile_live.shape, jnp.int32),
                pltpu.VMEM(day_factors.shape, jnp.bfloat16),
                pltpu.SMEM(tile_index.shape, jnp.int32),
                pltpu.SMEM(tile_live.shape, jnp.int32),
                pltpu.VMEM(day_factors.shape, jnp.bfloat16),
                pltpu.SMEM((blocks,), jnp.int32),
                pltpu.SemaphoreType.DMA((8,)),
            ],
            compiler_params=pltpu.CompilerParams(vmem_limit_bytes=PLAN_MIB * MIB),
        )(
            tile_index, tile_live, day_factors, mate_index, mate_live, mate_days, item_factors, tile_counts
        )
        kept, sent = pl.pallas_call(
            tiles_kernel,
            out_shape=(jax.ShapeDtypeStruct((devices // 2, own, rank), jnp.float32),) * 2,
            in_specs=[HBM, HBM, HBM, VMEM, VMEM, VMEM, VMEM],
            out_specs=(VMEM, VMEM),
            scratch_shapes=[
                pltpu.SMEM(plan_shape, jnp.int32),
                pltpu.VMEM((cap + 2 * CHUNK, *tile_counts.shape[1:]), jnp.bfloat16),
                pltpu.VMEM((blocks * TILE, rank), jnp.float32),
                pltpu.SemaphoreType.DMA,
                pltpu.SemaphoreType.DMA((cap // CHUNK + 2,)),
            ]
            + [pltpu.VMEM((GROUP * TILE, rank), jnp.bfloat16)] * UNROLL
            + [pltpu.VMEM((TILE, GROUP * TILE), jnp.bfloat16)] * UNROLL,
            compiler_params=pltpu.CompilerParams(vmem_limit_bytes=51 * MIB),
        )(plan, tile_counts, mate_counts, first_counts, gathered, items, day_rows)
        chip_sum = (kept + lax.ppermute(sent, "day", mates)).astype(jnp.bfloat16)
        extra = pl.pallas_call(
            functools.partial(sums_kernel, n_day // 2),
            out_shape=jax.ShapeDtypeStruct((8, LANES), jnp.bfloat16),
            in_specs=[ANY, VMEM, VMEM],
            out_specs=VMEM,
            compiler_params=pltpu.CompilerParams(vmem_limit_bytes=16 * MIB),
        )(kept, items, day_rows)
        sums = jnp.broadcast_to(extra[None], (devices // 2, 8, LANES))
        received = lax.all_to_all(
            jnp.concatenate([chip_sum, sums], axis=2),
            axes,
            0,
            0,
            axis_index_groups=[list(range(c, devices, 2)) for c in range(2)],
            tiled=True,
        )
        return pl.pallas_call(
            functools.partial(finish_kernel, n_item, n_day // 2),
            out_shape=jax.ShapeDtypeStruct((own, rank), jnp.float32),
            in_specs=[VMEM, VMEM],
            out_specs=VMEM,
            compiler_params=pltpu.CompilerParams(vmem_limit_bytes=16 * MIB),
        )(received, user_factors)

    in_specs = (
        P(axes, None),
        P("item", None),
        P("day", None),
        P(axes, None, None),
        P(None, axes),
        P(axes),
    )
    return jax.shard_map(
        per_device, mesh=mesh, in_specs=in_specs, out_specs=P(axes, None), check_vma=False
    )
```

```python
import functools

import jax
import jax.numpy as jnp
from jax import lax
from jax.experimental import pallas as pl
from jax.experimental.pallas import tpu as pltpu
from jax.sharding import PartitionSpec as P

TILE = 128
GROUP = 4
UNROLL = 4
CHUNK = 16
LANES = 128
NEEDS = 8
DAY_ROW = 4
FIRST = 3
PLAN_MIB = 50
VMEM = pl.BlockSpec(memory_space=pltpu.VMEM)
SMEM = pl.BlockSpec(memory_space=pltpu.SMEM)
ANY = pl.BlockSpec(memory_space=pl.ANY)
HBM = pl.BlockSpec(memory_space=pltpu.HBM)
MIB = 1024 * 1024


def round_up(n, m):
    return (n + m - 1) // m * m


def plan_kernel(
    blocks, live, mate_live, index, mate_index, mate_days, days_far, items_far, counts_far,
    plan, items, across, day_rows, first_counts,
    days, sems,
):
    fetch = [
        pltpu.make_async_copy(far, near, sems.at[i])
        for i, (far, near) in enumerate(
            (
                (days_far, days),
                (items_far, items),
                (counts_far.at[pl.ds(0, first_counts.shape[0])], first_counts),
            )
        )
    ]
    for copy in fetch:
        copy.start()

    mine, other = live[0], mate_live[0]
    half = (mine + other + 1) >> 1
    keep, mate_keep = jnp.minimum(mine, half), jnp.minimum(other, half)
    parts = jnp.maximum((keep + CHUNK - 1) // CHUNK, FIRST)
    mate_first = mate_keep // CHUNK
    mate_parts = jnp.where(mate_keep < other, (other + CHUNK - 1) // CHUNK - mate_first, 0)

    def iota(rows, columns, axis):
        return lax.broadcasted_iota(jnp.int32, (rows, columns), axis)

    def both(row):
        return jnp.concatenate([index[row : row + 1, :], mate_index[row : row + 1, :]], axis=1)

    cap = index.shape[1]
    wide = 2 * cap
    lane = iota(1, wide, 1)
    from_mate = lane >= cap
    slot = jnp.where(from_mate, lane - cap, lane)
    low, high = jnp.where(from_mate, mate_keep, 0), jnp.where(from_mate, other, keep)
    active = (slot >= low) & (slot < high)
    tile = slot + jnp.where(from_mate, (parts - mate_first) * CHUNK, 0)
    day = both(2) + jnp.where(from_mate, day_rows.shape[0] // 2, 0)
    user = jnp.where(active, both(0), -1)

    height = round_up(blocks, 16)
    hot = jnp.where(iota(height, wide, 0) == user, 1.0, 0.0)
    earlier = jnp.where(iota(wide, wide, 0) < iota(wide, wide, 1), 1.0, 0.0)
    rank = jnp.dot(
        hot.astype(jnp.bfloat16), earlier.astype(jnp.bfloat16), preferred_element_type=jnp.float32
    )
    sizes = jnp.sum(hot, axis=1, keepdims=True).astype(jnp.int32)
    groups = ((sizes + GROUP - 1) // GROUP).astype(jnp.float32)
    below = jnp.where(iota(height, height, 1) < iota(height, height, 0), 1.0, 0.0)
    before = jnp.dot(
        below.astype(jnp.bfloat16),
        jnp.broadcast_to(groups, (height, LANES)).astype(jnp.bfloat16),
        preferred_element_type=jnp.float32,
    )[:, 0:1]
    spot = jnp.sum(hot * (GROUP * before + rank), axis=0, keepdims=True).astype(jnp.int32)
    spot = jnp.where(active, spot, -1)

    rows = plan.shape[0] - 1
    taken = jnp.where(iota(rows * LANES, wide, 0) == spot, 1.0, 0.0).astype(jnp.bfloat16)
    field = iota(16, wide, 0)
    fields = jnp.zeros((16, wide), jnp.int32)
    for k, value in enumerate((user, tile, both(1), day, jnp.ones_like(user))):
        fields = jnp.where(field == k, value, fields)
    found = lax.dot_general(
        fields.astype(jnp.float32).astype(jnp.bfloat16),
        taken,
        (((1,), (1,)), ((), ())),
        preferred_element_type=jnp.float32,
    ).astype(jnp.int32)
    code = (found[0:1] << 24) | (found[1:2] << 16) | (found[2:3] << 8) | found[3:4]
    code = jnp.where(found[4:5] > 0, code, -1)
    for k in range(rows):
        plan[1 + k : 2 + k, :] = code[:, k * LANES : (k + 1) * LANES]

    turns = round_up(rows * LANES // (GROUP * UNROLL), 8)
    turn = jnp.floor((spot.astype(jnp.float32) + 0.5) / (GROUP * UNROLL)).astype(jnp.int32)
    in_turn = iota(turns, wide, 0) == jnp.where(active, turn, -1)
    need = jnp.max(jnp.where(in_turn, tile // CHUNK + 1, 0), axis=1, keepdims=True)
    at = iota(1, LANES, 1)
    head = jnp.sum(
        jnp.where(iota(turns, LANES, 1) == iota(turns, LANES, 0) + NEEDS, need, 0),
        axis=0,
        keepdims=True,
    )
    head = jnp.where(at == 0, jnp.sum(groups, axis=0, keepdims=True).astype(jnp.int32), head)
    for k, value in ((1, parts), (2, mate_first), (3, parts + mate_parts)):
        head = jnp.where(at == k, value, head)
    plan[0:1, :] = head

    fetch[0].wait()
    day_rows[...] = jnp.zeros_like(day_rows)
    count, space = days.shape[0], day_rows.shape[0] // 2
    day_rows[0:count, :] = days[...].astype(jnp.float32)
    day_rows[space : space + count, :] = mate_days[...].astype(jnp.float32)
    fetch[1].wait()
    across[...] = items[...].astype(jnp.float32).T.astype(jnp.bfloat16)
    fetch[2].wait()


def sums_kernel(chips, kept, items, day_rows, extra):
    rank = items.shape[1]
    day_sum = jnp.sum(day_rows[...], axis=0, keepdims=True)
    item_sum = jnp.sum(items[...].astype(jnp.float32), axis=0, keepdims=True)
    item_at, chip_at = lax.axis_index("item"), lax.axis_index("day") >> 1
    row = lax.broadcasted_iota(jnp.int32, (8, LANES), 0)
    block = jnp.zeros((8, LANES), jnp.float32)
    for q in range(rank // LANES):
        for first, total, here in (
            (2 * (q // chips), item_sum, chip_at == q % chips),
            (DAY_ROW, day_sum, item_at == q),
        ):
            part = jnp.where(here, total[:, q * LANES : (q + 1) * LANES], 0.0)
            high = part.astype(jnp.bfloat16).astype(jnp.float32)
            block = jnp.where(row == first, block + high, block)
            block = jnp.where(row == first + 1, block + (part - high), block)
    extra[...] = block.astype(jnp.bfloat16)


def tiles_kernel(
    plan_far, counts_far, mate_counts_far, first_counts, users, items, across, day_rows,
    kept, sent,
    plan, counts, phi, plan_sem, counts_sem, *buffers,
):
    weighted, ratios = buffers[:UNROLL], buffers[UNROLL:]
    fetch = pltpu.make_async_copy(plan_far, plan, plan_sem)
    fetch.start()

    def part(far, c, at):
        source = far.at[pl.ds(pl.multiple_of(c * CHUNK, CHUNK), CHUNK)]
        target = counts.at[pl.ds(pl.multiple_of(at * CHUNK, CHUNK), CHUNK)]
        return pltpu.make_async_copy(source, target, counts_sem.at[at])

    counts[0 : FIRST * CHUNK] = first_counts[...]
    phi[...] = jnp.zeros_like(phi)
    weighted[-1][...] = jnp.zeros_like(weighted[-1])
    ratios[-1][...] = jnp.zeros_like(ratios[-1])
    fetch.wait()
    groups, parts, mate_first, all_parts = plan[0, 0], plan[0, 1], plan[0, 2], plan[0, 3]

    def start_part(c, carry):
        part(counts_far, c, c).start()
        return carry

    def start_mate_part(c, carry):
        part(mate_counts_far, mate_first + c - parts, c).start()
        return carry

    def wait_part(c, carry):
        part(counts_far, 0, c).wait()
        return carry

    lax.fori_loop(FIRST, parts, start_part, 0)
    lax.fori_loop(parts, all_parts, start_mate_part, 0)

    def code_at(spot):
        return plan[1 + (spot >> 7), spot & (LANES - 1)]

    def block_of(g):
        return pl.ds(pl.multiple_of((jnp.maximum(code_at(g * GROUP), 0) >> 24) * TILE, TILE), TILE)

    def make_ratio(g, i):
        rows = users[block_of(g), :]
        codes = [code_at(g * GROUP + j) for j in range(GROUP)]
        slots = [jnp.maximum(code, 0) for code in codes]
        for j, slot in enumerate(slots):
            item = pl.multiple_of(((slot >> 8) & 255) * TILE, TILE)
            scale = day_rows[pl.ds(slot & 255, 1), :].astype(jnp.bfloat16)
            weighted[i][j * TILE : (j + 1) * TILE, :] = items[pl.ds(item, TILE), :] * scale
            model = jnp.dot(
                rows * scale, across[:, pl.ds(item, TILE)], preferred_element_type=jnp.float32
            )
            ratio = counts[(slot >> 16) & 255].astype(jnp.float32) / model
            ratios[i][:, j * TILE : (j + 1) * TILE] = jnp.where(codes[j] >= 0, ratio, 0.0).astype(
                jnp.bfloat16
            )

    def add_terms(g, i):
        phi[block_of(g), :] += jnp.dot(
            ratios[i][...], weighted[i][...], preferred_element_type=jnp.float32
        )

    def turn(t, ready):
        need = jnp.maximum(plan[0, NEEDS + t], ready)
        lax.fori_loop(ready, need, wait_part, 0)
        for i in range(UNROLL):
            g = t * UNROLL + i
            make_ratio(g, i)
            add_terms(jnp.maximum(g - 1, 0), (i - 1) % UNROLL)
        return need

    turns = (groups + UNROLL - 2) // UNROLL
    ready = lax.fori_loop(0, turns, turn, jnp.int32(FIRST))
    lax.fori_loop(ready, all_parts, wait_part, 0)
    add_terms(jnp.maximum(turns * UNROLL - 1, 0), UNROLL - 1)

    @pl.when(groups > turns * UNROLL)
    def _():
        make_ratio(turns * UNROLL, 0)
        add_terms(turns * UNROLL, 0)

    own = kept.shape[1]
    core = lax.axis_index("day") & 1
    for j in range(kept.shape[0]):
        kept[j] = phi[pl.ds(pl.multiple_of((2 * j + core) * own, own), own), :]
        sent[j] = phi[pl.ds(pl.multiple_of((2 * j + 1 - core) * own, own), own), :]


def finish_kernel(n_item, chips, received, user_factors, out):
    rank = user_factors.shape[1]
    phi = jnp.sum(received[:, :, 0:rank].astype(jnp.float32), axis=0)
    for q in range(rank // LANES):
        cols = slice(q * LANES, (q + 1) * LANES)
        item = received[q % chips, :, rank:].astype(jnp.float32)
        for i in range(1, n_item):
            item = item + received[i * chips + q % chips, :, rank:].astype(jnp.float32)
        day = received[q * chips, :, rank:].astype(jnp.float32)
        for k in range(1, chips):
            day = day + received[q * chips + k, :, rank:].astype(jnp.float32)
        at = 2 * (q // chips)
        totals = (item[at : at + 1] + item[at + 1 : at + 2]) * (
            day[DAY_ROW : DAY_ROW + 1] + day[DAY_ROW + 1 : DAY_ROW + 2]
        )
        out[:, cols] = user_factors[:, cols] * phi[:, cols] / totals


def solution(mesh):
    n_item, n_day = mesh.shape["item"], mesh.shape["day"]
    devices = n_item * n_day
    axes = ("item", "day")
    mates = [(k, k ^ 1) for k in range(n_day)]

    def per_device(user_factors, item_factors, day_factors, tile_counts, tile_index, tile_live):
        own, rank = user_factors.shape
        blocks = own * devices // TILE
        cap = tile_counts.shape[0]
        day_space = round_up(day_factors.shape[0], 8)
        groups = round_up(cap // GROUP + blocks, UNROLL)
        plan_shape = (1 + pl.cdiv(groups * GROUP, LANES), LANES)
        mate_counts, mate_index, mate_live, mate_days = (
            lax.ppermute(x, "day", mates)
            for x in (tile_counts, tile_index, tile_live, day_factors)
        )
        spread = jnp.broadcast_to(user_factors.astype(jnp.bfloat16)[None], (devices, own, rank))
        gathered = lax.all_to_all(spread, axes, 0, 0, tiled=True).reshape(devices * own, rank)
        plan, items, across, day_rows, first_counts = pl.pallas_call(
            functools.partial(plan_kernel, blocks),
            out_shape=(
                jax.ShapeDtypeStruct(plan_shape, jnp.int32),
                jax.ShapeDtypeStruct(item_factors.shape, jnp.bfloat16),
                jax.ShapeDtypeStruct(item_factors.shape[::-1], jnp.bfloat16),
                jax.ShapeDtypeStruct((2 * day_space, rank), jnp.float32),
                jax.ShapeDtypeStruct((FIRST * CHUNK, *tile_counts.shape[1:]), jnp.bfloat16),
            ),
            in_specs=[SMEM, SMEM, VMEM, VMEM, VMEM, HBM, HBM, HBM],
            out_specs=(VMEM, VMEM, VMEM, VMEM, VMEM),
            scratch_shapes=[
                pltpu.VMEM(day_factors.shape, jnp.bfloat16),
                pltpu.SemaphoreType.DMA((3,)),
            ],
            compiler_params=pltpu.CompilerParams(vmem_limit_bytes=PLAN_MIB * MIB),
        )(
            tile_live, mate_live, tile_index, mate_index, mate_days,
            day_factors, item_factors, tile_counts,
        )
        kept, sent = pl.pallas_call(
            tiles_kernel,
            out_shape=(jax.ShapeDtypeStruct((devices // 2, own, rank), jnp.float32),) * 2,
            in_specs=[HBM, HBM, HBM, VMEM, VMEM, VMEM, VMEM, VMEM],
            out_specs=(VMEM, VMEM),
            scratch_shapes=[
                pltpu.SMEM(plan_shape, jnp.int32),
                pltpu.VMEM((cap + 2 * CHUNK, *tile_counts.shape[1:]), jnp.bfloat16),
                pltpu.VMEM((blocks * TILE, rank), jnp.float32),
                pltpu.SemaphoreType.DMA,
                pltpu.SemaphoreType.DMA((cap // CHUNK + 2,)),
            ]
            + [pltpu.VMEM((GROUP * TILE, rank), jnp.bfloat16)] * UNROLL
            + [pltpu.VMEM((TILE, GROUP * TILE), jnp.bfloat16)] * UNROLL,
            compiler_params=pltpu.CompilerParams(vmem_limit_bytes=50 * MIB),
        )(plan, tile_counts, mate_counts, first_counts, gathered, items, across, day_rows)
        chip_sum = (kept + lax.ppermute(sent, "day", mates)).astype(jnp.bfloat16)
        extra = pl.pallas_call(
            functools.partial(sums_kernel, n_day // 2),
            out_shape=jax.ShapeDtypeStruct((8, LANES), jnp.bfloat16),
            in_specs=[ANY, VMEM, VMEM],
            out_specs=VMEM,
            compiler_params=pltpu.CompilerParams(vmem_limit_bytes=16 * MIB),
        )(kept, items, day_rows)
        sums = jnp.broadcast_to(extra[None], (devices // 2, 8, LANES))
        received = lax.all_to_all(
            jnp.concatenate([chip_sum, sums], axis=2),
            axes,
            0,
            0,
            axis_index_groups=[list(range(c, devices, 2)) for c in range(2)],
            tiled=True,
        )
        return pl.pallas_call(
            functools.partial(finish_kernel, n_item, n_day // 2),
            out_shape=jax.ShapeDtypeStruct((own, rank), jnp.float32),
            in_specs=[VMEM, VMEM],
            out_specs=VMEM,
            compiler_params=pltpu.CompilerParams(vmem_limit_bytes=16 * MIB),
        )(received, user_factors)

    in_specs = (
        P(axes, None),
        P("item", None),
        P("day", None),
        P(axes, None, None),
        P(None, axes),
        P(axes),
    )
    return jax.shard_map(
        per_device, mesh=mesh, in_specs=in_specs, out_specs=P(axes, None), check_vma=False
    )
```

```python
import functools

import jax
import jax.numpy as jnp
from jax import lax
from jax.experimental import pallas as pl
from jax.experimental.pallas import tpu as pltpu
from jax.sharding import PartitionSpec as P

TILE = 128
GROUP = 4
UNROLL = 5
TAIL = 2
CHUNK = 16
LANES = 128
NEEDS = 8
DAY_ROW = 4
FIRST = 3
PLAN_MIB = 50
VMEM = pl.BlockSpec(memory_space=pltpu.VMEM)
SMEM = pl.BlockSpec(memory_space=pltpu.SMEM)
ANY = pl.BlockSpec(memory_space=pl.ANY)
HBM = pl.BlockSpec(memory_space=pltpu.HBM)
MIB = 1024 * 1024


def round_up(n, m):
    return (n + m - 1) // m * m


def plan_kernel(
    blocks, live, mate_live, index, mate_index, mate_days, days_far, items_far, counts_far,
    plan, items, across, day_rows, first_counts,
    days, sems,
):
    fetch = [
        pltpu.make_async_copy(far, near, sems.at[i])
        for i, (far, near) in enumerate(
            (
                (days_far, days),
                (items_far, items),
                (counts_far.at[pl.ds(0, first_counts.shape[0])], first_counts),
            )
        )
    ]
    for copy in fetch:
        copy.start()

    mine, other = live[0], mate_live[0]
    half = (mine + other + 1) >> 1
    keep, mate_keep = jnp.minimum(mine, half), jnp.minimum(other, half)
    parts = jnp.maximum((keep + CHUNK - 1) // CHUNK, FIRST)
    mate_first = mate_keep // CHUNK
    mate_parts = jnp.where(mate_keep < other, (other + CHUNK - 1) // CHUNK - mate_first, 0)

    def iota(rows, columns, axis):
        return lax.broadcasted_iota(jnp.int32, (rows, columns), axis)

    def both(row):
        return jnp.concatenate([index[row : row + 1, :], mate_index[row : row + 1, :]], axis=1)

    cap = index.shape[1]
    wide = 2 * cap
    lane = iota(1, wide, 1)
    from_mate = lane >= cap
    slot = jnp.where(from_mate, lane - cap, lane)
    low, high = jnp.where(from_mate, mate_keep, 0), jnp.where(from_mate, other, keep)
    active = (slot >= low) & (slot < high)
    tile = slot + jnp.where(from_mate, (parts - mate_first) * CHUNK, 0)
    day = both(2) + jnp.where(from_mate, day_rows.shape[0] // 2, 0)
    user = jnp.where(active, both(0), -1)

    height = round_up(blocks, 16)
    hot = jnp.where(iota(height, wide, 0) == user, 1.0, 0.0)
    earlier = jnp.where(iota(wide, wide, 0) < iota(wide, wide, 1), 1.0, 0.0)
    rank = jnp.dot(
        hot.astype(jnp.bfloat16), earlier.astype(jnp.bfloat16), preferred_element_type=jnp.float32
    )
    sizes = jnp.sum(hot, axis=1, keepdims=True).astype(jnp.int32)
    groups = ((sizes + GROUP - 1) // GROUP).astype(jnp.float32)
    below = jnp.where(iota(height, height, 1) < iota(height, height, 0), 1.0, 0.0)
    before = jnp.dot(
        below.astype(jnp.bfloat16),
        jnp.broadcast_to(groups, (height, LANES)).astype(jnp.bfloat16),
        preferred_element_type=jnp.float32,
    )[:, 0:1]
    spot = jnp.sum(hot * (GROUP * before + rank), axis=0, keepdims=True).astype(jnp.int32)
    spot = jnp.where(active, spot, -1)

    rows = plan.shape[0] - 1
    taken = jnp.where(iota(rows * LANES, wide, 0) == spot, 1.0, 0.0).astype(jnp.bfloat16)
    field = iota(16, wide, 0)
    fields = jnp.zeros((16, wide), jnp.int32)
    for k, value in enumerate((user, tile, both(1), day, jnp.ones_like(user))):
        fields = jnp.where(field == k, value, fields)
    found = lax.dot_general(
        fields.astype(jnp.float32).astype(jnp.bfloat16),
        taken,
        (((1,), (1,)), ((), ())),
        preferred_element_type=jnp.float32,
    ).astype(jnp.int32)
    code = (found[0:1] << 24) | (found[1:2] << 16) | (found[2:3] << 8) | found[3:4]
    code = jnp.where(found[4:5] > 0, code, -1)
    for k in range(rows):
        plan[1 + k : 2 + k, :] = code[:, k * LANES : (k + 1) * LANES]

    turns = round_up(rows * LANES // (GROUP * UNROLL), 8)
    turn = jnp.floor((spot.astype(jnp.float32) + 0.5) / (GROUP * UNROLL)).astype(jnp.int32)
    in_turn = iota(turns, wide, 0) == jnp.where(active, turn, -1)
    need = jnp.max(jnp.where(in_turn, tile // CHUNK + 1, 0), axis=1, keepdims=True)
    at = iota(1, LANES, 1)
    head = jnp.sum(
        jnp.where(iota(turns, LANES, 1) == iota(turns, LANES, 0) + NEEDS, need, 0),
        axis=0,
        keepdims=True,
    )
    head = jnp.where(at == 0, jnp.sum(groups, axis=0, keepdims=True).astype(jnp.int32), head)
    for k, value in ((1, parts), (2, mate_first), (3, parts + mate_parts)):
        head = jnp.where(at == k, value, head)
    plan[0:1, :] = head

    fetch[0].wait()
    day_rows[...] = jnp.zeros_like(day_rows)
    count, space = days.shape[0], day_rows.shape[0] // 2
    day_rows[0:count, :] = days[...].astype(jnp.float32)
    day_rows[space : space + count, :] = mate_days[...].astype(jnp.float32)
    fetch[1].wait()
    across[...] = items[...].astype(jnp.float32).T.astype(jnp.bfloat16)
    fetch[2].wait()


def sums_kernel(chips, kept, items, day_rows, extra):
    rank = items.shape[1]
    day_sum = jnp.sum(day_rows[...], axis=0, keepdims=True)
    item_sum = jnp.sum(items[...].astype(jnp.float32), axis=0, keepdims=True)
    item_at, chip_at = lax.axis_index("item"), lax.axis_index("day") >> 1
    row = lax.broadcasted_iota(jnp.int32, (8, LANES), 0)
    block = jnp.zeros((8, LANES), jnp.float32)
    for q in range(rank // LANES):
        for first, total, here in (
            (2 * (q // chips), item_sum, chip_at == q % chips),
            (DAY_ROW, day_sum, item_at == q),
        ):
            part = jnp.where(here, total[:, q * LANES : (q + 1) * LANES], 0.0)
            high = part.astype(jnp.bfloat16).astype(jnp.float32)
            block = jnp.where(row == first, block + high, block)
            block = jnp.where(row == first + 1, block + (part - high), block)
    extra[...] = block.astype(jnp.bfloat16)


def tiles_kernel(
    plan_far, counts_far, mate_counts_far, first_counts, users, items, across, day_rows,
    kept, sent,
    plan, counts, phi, plan_sem, counts_sem, *buffers,
):
    weighted, ratios = buffers[:UNROLL], buffers[UNROLL:]
    fetch = pltpu.make_async_copy(plan_far, plan, plan_sem)
    fetch.start()

    def part(far, c, at):
        source = far.at[pl.ds(pl.multiple_of(c * CHUNK, CHUNK), CHUNK)]
        target = counts.at[pl.ds(pl.multiple_of(at * CHUNK, CHUNK), CHUNK)]
        return pltpu.make_async_copy(source, target, counts_sem.at[at])

    counts[0 : FIRST * CHUNK] = first_counts[...]
    phi[...] = jnp.zeros_like(phi)
    weighted[-1][...] = jnp.zeros_like(weighted[-1])
    ratios[-1][...] = jnp.zeros_like(ratios[-1])
    fetch.wait()
    groups, parts, mate_first, all_parts = plan[0, 0], plan[0, 1], plan[0, 2], plan[0, 3]

    def start_part(c, carry):
        part(counts_far, c, c).start()
        return carry

    def start_mate_part(c, carry):
        part(mate_counts_far, mate_first + c - parts, c).start()
        return carry

    def wait_part(c, carry):
        part(counts_far, 0, c).wait()
        return carry

    lax.fori_loop(FIRST, parts, start_part, 0)
    lax.fori_loop(parts, all_parts, start_mate_part, 0)

    def code_at(spot):
        return plan[1 + (spot >> 7), spot & (LANES - 1)]

    def block_of(g):
        return pl.ds(pl.multiple_of((jnp.maximum(code_at(g * GROUP), 0) >> 24) * TILE, TILE), TILE)

    def make_ratio(g, i):
        rows = users[block_of(g), :]
        codes = [code_at(g * GROUP + j) for j in range(GROUP)]
        slots = [jnp.maximum(code, 0) for code in codes]
        for j, slot in enumerate(slots):
            item = pl.multiple_of(((slot >> 8) & 255) * TILE, TILE)
            scale = day_rows[pl.ds(slot & 255, 1), :].astype(jnp.bfloat16)
            weighted[i][j * TILE : (j + 1) * TILE, :] = items[pl.ds(item, TILE), :] * scale
            model = jnp.dot(
                rows * scale, across[:, pl.ds(item, TILE)], preferred_element_type=jnp.float32
            )
            ratio = counts[(slot >> 16) & 255].astype(jnp.float32) / model
            ratios[i][:, j * TILE : (j + 1) * TILE] = jnp.where(codes[j] >= 0, ratio, 0.0).astype(
                jnp.bfloat16
            )

    def add_terms(g, i):
        phi[block_of(g), :] += jnp.dot(
            ratios[i][...], weighted[i][...], preferred_element_type=jnp.float32
        )

    def turn(t, ready):
        need = jnp.maximum(plan[0, NEEDS + t], ready)
        lax.fori_loop(ready, need, wait_part, 0)
        for i in range(UNROLL):
            g = t * UNROLL + i
            make_ratio(g, i)
            add_terms(jnp.maximum(g - 1, 0), (i - 1) % UNROLL)
        return need

    turns = (groups + UNROLL - 1 - TAIL) // UNROLL
    ready = lax.fori_loop(0, turns, turn, jnp.int32(FIRST))
    lax.fori_loop(ready, all_parts, wait_part, 0)
    first = turns * UNROLL
    rest = groups - first

    def tail(count):
        for i in range(count):
            make_ratio(first + i, i)
            add_terms(jnp.maximum(first + i - 1, 0), (i - 1) % UNROLL)
        add_terms(jnp.maximum(first + count - 1, 0), (count - 1) % UNROLL)

    for count, chosen in ((0, rest <= 0), (1, rest == 1), (TAIL, rest > 1)):
        pl.when(chosen)(functools.partial(tail, count))

    own = kept.shape[1]
    core = lax.axis_index("day") & 1
    for j in range(kept.shape[0]):
        kept[j] = phi[pl.ds(pl.multiple_of((2 * j + core) * own, own), own), :]
        sent[j] = phi[pl.ds(pl.multiple_of((2 * j + 1 - core) * own, own), own), :]


def finish_kernel(n_item, chips, received, user_factors, out):
    rank = user_factors.shape[1]
    phi = jnp.sum(received[:, :, 0:rank].astype(jnp.float32), axis=0)
    for q in range(rank // LANES):
        cols = slice(q * LANES, (q + 1) * LANES)
        item = received[q % chips, :, rank:].astype(jnp.float32)
        for i in range(1, n_item):
            item = item + received[i * chips + q % chips, :, rank:].astype(jnp.float32)
        day = received[q * chips, :, rank:].astype(jnp.float32)
        for k in range(1, chips):
            day = day + received[q * chips + k, :, rank:].astype(jnp.float32)
        at = 2 * (q // chips)
        totals = (item[at : at + 1] + item[at + 1 : at + 2]) * (
            day[DAY_ROW : DAY_ROW + 1] + day[DAY_ROW + 1 : DAY_ROW + 2]
        )
        out[:, cols] = user_factors[:, cols] * phi[:, cols] / totals


def solution(mesh):
    n_item, n_day = mesh.shape["item"], mesh.shape["day"]
    devices = n_item * n_day
    axes = ("item", "day")
    mates = [(k, k ^ 1) for k in range(n_day)]

    def per_device(user_factors, item_factors, day_factors, tile_counts, tile_index, tile_live):
        own, rank = user_factors.shape
        blocks = own * devices // TILE
        cap = tile_counts.shape[0]
        day_space = round_up(day_factors.shape[0], 8)
        groups = round_up(cap // GROUP + blocks, UNROLL)
        plan_shape = (1 + pl.cdiv(groups * GROUP, LANES), LANES)
        mate_counts, mate_index, mate_live, mate_days = (
            lax.ppermute(x, "day", mates)
            for x in (tile_counts, tile_index, tile_live, day_factors)
        )
        spread = jnp.broadcast_to(user_factors.astype(jnp.bfloat16)[None], (devices, own, rank))
        gathered = lax.all_to_all(spread, axes, 0, 0, tiled=True).reshape(devices * own, rank)
        plan, items, across, day_rows, first_counts = pl.pallas_call(
            functools.partial(plan_kernel, blocks),
            out_shape=(
                jax.ShapeDtypeStruct(plan_shape, jnp.int32),
                jax.ShapeDtypeStruct(item_factors.shape, jnp.bfloat16),
                jax.ShapeDtypeStruct(item_factors.shape[::-1], jnp.bfloat16),
                jax.ShapeDtypeStruct((2 * day_space, rank), jnp.float32),
                jax.ShapeDtypeStruct((FIRST * CHUNK, *tile_counts.shape[1:]), jnp.bfloat16),
            ),
            in_specs=[SMEM, SMEM, VMEM, VMEM, VMEM, HBM, HBM, HBM],
            out_specs=(VMEM, VMEM, VMEM, VMEM, VMEM),
            scratch_shapes=[
                pltpu.VMEM(day_factors.shape, jnp.bfloat16),
                pltpu.SemaphoreType.DMA((3,)),
            ],
            compiler_params=pltpu.CompilerParams(vmem_limit_bytes=PLAN_MIB * MIB),
        )(
            tile_live, mate_live, tile_index, mate_index, mate_days,
            day_factors, item_factors, tile_counts,
        )
        kept, sent = pl.pallas_call(
            tiles_kernel,
            out_shape=(jax.ShapeDtypeStruct((devices // 2, own, rank), jnp.float32),) * 2,
            in_specs=[HBM, HBM, HBM, VMEM, VMEM, VMEM, VMEM, VMEM],
            out_specs=(VMEM, VMEM),
            scratch_shapes=[
                pltpu.SMEM(plan_shape, jnp.int32),
                pltpu.VMEM((cap + 2 * CHUNK, *tile_counts.shape[1:]), jnp.bfloat16),
                pltpu.VMEM((blocks * TILE, rank), jnp.float32),
                pltpu.SemaphoreType.DMA,
                pltpu.SemaphoreType.DMA((cap // CHUNK + 2,)),
            ]
            + [pltpu.VMEM((GROUP * TILE, rank), jnp.bfloat16)] * UNROLL
            + [pltpu.VMEM((TILE, GROUP * TILE), jnp.bfloat16)] * UNROLL,
            compiler_params=pltpu.CompilerParams(vmem_limit_bytes=50 * MIB),
        )(plan, tile_counts, mate_counts, first_counts, gathered, items, across, day_rows)
        chip_sum = (kept + lax.ppermute(sent, "day", mates)).astype(jnp.bfloat16)
        extra = pl.pallas_call(
            functools.partial(sums_kernel, n_day // 2),
            out_shape=jax.ShapeDtypeStruct((8, LANES), jnp.bfloat16),
            in_specs=[ANY, VMEM, VMEM],
            out_specs=VMEM,
            compiler_params=pltpu.CompilerParams(vmem_limit_bytes=16 * MIB),
        )(kept, items, day_rows)
        sums = jnp.broadcast_to(extra[None], (devices // 2, 8, LANES))
        received = lax.all_to_all(
            jnp.concatenate([chip_sum, sums], axis=2),
            axes,
            0,
            0,
            axis_index_groups=[list(range(c, devices, 2)) for c in range(2)],
            tiled=True,
        )
        return pl.pallas_call(
            functools.partial(finish_kernel, n_item, n_day // 2),
            out_shape=jax.ShapeDtypeStruct((own, rank), jnp.float32),
            in_specs=[VMEM, VMEM],
            out_specs=VMEM,
            compiler_params=pltpu.CompilerParams(vmem_limit_bytes=16 * MIB),
        )(received, user_factors)

    in_specs = (
        P(axes, None),
        P("item", None),
        P("day", None),
        P(axes, None, None),
        P(None, axes),
        P(axes),
    )
    return jax.shard_map(
        per_device, mesh=mesh, in_specs=in_specs, out_specs=P(axes, None), check_vma=False
    )
```

```python
import functools

import jax
import jax.numpy as jnp
from jax import lax
from jax.experimental import pallas as pl
from jax.experimental.pallas import tpu as pltpu
from jax.sharding import PartitionSpec as P

TILE = 128
GROUP = 4
UNROLL = 4
TAIL = 3
CHUNK = 16
LANES = 128
NEEDS = 8
DAY_ROW = 4
FIRST = 3
PLAN_MIB = 50
VMEM = pl.BlockSpec(memory_space=pltpu.VMEM)
SMEM = pl.BlockSpec(memory_space=pltpu.SMEM)
ANY = pl.BlockSpec(memory_space=pl.ANY)
HBM = pl.BlockSpec(memory_space=pltpu.HBM)
MIB = 1024 * 1024


def round_up(n, m):
    return (n + m - 1) // m * m


def plan_kernel(
    blocks, live, mate_live, index, mate_index, mate_days, days_far, items_far, counts_far,
    plan, items, across, day_rows, first_counts,
    days, sems,
):
    fetch = [
        pltpu.make_async_copy(far, near, sems.at[i])
        for i, (far, near) in enumerate(
            (
                (days_far, days),
                (items_far, items),
                (counts_far.at[pl.ds(0, first_counts.shape[0])], first_counts),
            )
        )
    ]
    for copy in fetch:
        copy.start()

    mine, other = live[0], mate_live[0]
    half = (mine + other + 1) >> 1
    keep, mate_keep = jnp.minimum(mine, half), jnp.minimum(other, half)
    parts = jnp.maximum((keep + CHUNK - 1) // CHUNK, FIRST)
    mate_first = mate_keep // CHUNK
    mate_parts = jnp.where(mate_keep < other, (other + CHUNK - 1) // CHUNK - mate_first, 0)

    def iota(rows, columns, axis):
        return lax.broadcasted_iota(jnp.int32, (rows, columns), axis)

    def both(row):
        return jnp.concatenate([index[row : row + 1, :], mate_index[row : row + 1, :]], axis=1)

    cap = index.shape[1]
    wide = 2 * cap
    lane = iota(1, wide, 1)
    from_mate = lane >= cap
    slot = jnp.where(from_mate, lane - cap, lane)
    low, high = jnp.where(from_mate, mate_keep, 0), jnp.where(from_mate, other, keep)
    active = (slot >= low) & (slot < high)
    tile = slot + jnp.where(from_mate, (parts - mate_first) * CHUNK, 0)
    day = both(2) + jnp.where(from_mate, day_rows.shape[0] // 2, 0)
    user = jnp.where(active, both(0), -1)

    height = round_up(blocks, 16)
    hot = jnp.where(iota(height, wide, 0) == user, 1.0, 0.0)
    earlier = jnp.where(iota(wide, wide, 0) < iota(wide, wide, 1), 1.0, 0.0)
    rank = jnp.dot(
        hot.astype(jnp.bfloat16), earlier.astype(jnp.bfloat16), preferred_element_type=jnp.float32
    )
    sizes = jnp.sum(hot, axis=1, keepdims=True).astype(jnp.int32)
    groups = ((sizes + GROUP - 1) // GROUP).astype(jnp.float32)
    below = jnp.where(iota(height, height, 1) < iota(height, height, 0), 1.0, 0.0)
    before = jnp.dot(
        below.astype(jnp.bfloat16),
        jnp.broadcast_to(groups, (height, LANES)).astype(jnp.bfloat16),
        preferred_element_type=jnp.float32,
    )[:, 0:1]
    spot = jnp.sum(hot * (GROUP * before + rank), axis=0, keepdims=True).astype(jnp.int32)
    spot = jnp.where(active, spot, -1)

    rows = plan.shape[0] - 1
    taken = jnp.where(iota(rows * LANES, wide, 0) == spot, 1.0, 0.0).astype(jnp.bfloat16)
    field = iota(16, wide, 0)
    fields = jnp.zeros((16, wide), jnp.int32)
    for k, value in enumerate((user, tile, both(1), day, jnp.ones_like(user))):
        fields = jnp.where(field == k, value, fields)
    found = lax.dot_general(
        fields.astype(jnp.float32).astype(jnp.bfloat16),
        taken,
        (((1,), (1,)), ((), ())),
        preferred_element_type=jnp.float32,
    ).astype(jnp.int32)
    code = (found[0:1] << 24) | (found[1:2] << 16) | (found[2:3] << 8) | found[3:4]
    code = jnp.where(found[4:5] > 0, code, -1)
    for k in range(rows):
        plan[1 + k : 2 + k, :] = code[:, k * LANES : (k + 1) * LANES]

    turns = round_up(rows * LANES // (GROUP * UNROLL), 8)
    turn = jnp.floor((spot.astype(jnp.float32) + 0.5) / (GROUP * UNROLL)).astype(jnp.int32)
    in_turn = iota(turns, wide, 0) == jnp.where(active, turn, -1)
    need = jnp.max(jnp.where(in_turn, tile // CHUNK + 1, 0), axis=1, keepdims=True)
    at = iota(1, LANES, 1)
    head = jnp.sum(
        jnp.where(iota(turns, LANES, 1) == iota(turns, LANES, 0) + NEEDS, need, 0),
        axis=0,
        keepdims=True,
    )
    head = jnp.where(at == 0, jnp.sum(groups, axis=0, keepdims=True).astype(jnp.int32), head)
    for k, value in ((1, parts), (2, mate_first), (3, parts + mate_parts)):
        head = jnp.where(at == k, value, head)
    plan[0:1, :] = head

    fetch[0].wait()
    day_rows[...] = jnp.zeros_like(day_rows)
    count, space = days.shape[0], day_rows.shape[0] // 2
    day_rows[0:count, :] = days[...].astype(jnp.float32)
    day_rows[space : space + count, :] = mate_days[...].astype(jnp.float32)
    fetch[1].wait()
    across[...] = items[...].astype(jnp.float32).T.astype(jnp.bfloat16)
    fetch[2].wait()


def sums_kernel(chips, kept, items, day_rows, extra):
    rank = items.shape[1]
    day_sum = jnp.sum(day_rows[...], axis=0, keepdims=True)
    item_sum = jnp.sum(items[...].astype(jnp.float32), axis=0, keepdims=True)
    item_at, chip_at = lax.axis_index("item"), lax.axis_index("day") >> 1
    row = lax.broadcasted_iota(jnp.int32, (8, LANES), 0)
    block = jnp.zeros((8, LANES), jnp.float32)
    for q in range(rank // LANES):
        for first, total, here in (
            (2 * (q // chips), item_sum, chip_at == q % chips),
            (DAY_ROW, day_sum, item_at == q),
        ):
            part = jnp.where(here, total[:, q * LANES : (q + 1) * LANES], 0.0)
            high = part.astype(jnp.bfloat16).astype(jnp.float32)
            block = jnp.where(row == first, block + high, block)
            block = jnp.where(row == first + 1, block + (part - high), block)
    extra[...] = block.astype(jnp.bfloat16)


def tiles_kernel(
    plan_far, counts_far, mate_counts_far, first_counts, users, items, across, day_rows,
    kept, sent,
    plan, counts, phi, plan_sem, counts_sem, *buffers,
):
    weighted, ratios = buffers[:UNROLL], buffers[UNROLL:]
    fetch = pltpu.make_async_copy(plan_far, plan, plan_sem)
    fetch.start()

    def part(far, c, at):
        source = far.at[pl.ds(pl.multiple_of(c * CHUNK, CHUNK), CHUNK)]
        target = counts.at[pl.ds(pl.multiple_of(at * CHUNK, CHUNK), CHUNK)]
        return pltpu.make_async_copy(source, target, counts_sem.at[at])

    counts[0 : FIRST * CHUNK] = first_counts[...]
    phi[...] = jnp.zeros_like(phi)
    weighted[-1][...] = jnp.zeros_like(weighted[-1])
    ratios[-1][...] = jnp.zeros_like(ratios[-1])
    fetch.wait()
    groups, parts, mate_first, all_parts = plan[0, 0], plan[0, 1], plan[0, 2], plan[0, 3]

    def start_part(c, carry):
        part(counts_far, c, c).start()
        return carry

    def start_mate_part(c, carry):
        part(mate_counts_far, mate_first + c - parts, c).start()
        return carry

    def wait_part(c, carry):
        part(counts_far, 0, c).wait()
        return carry

    lax.fori_loop(FIRST, parts, start_part, 0)
    lax.fori_loop(parts, all_parts, start_mate_part, 0)

    def code_at(spot):
        return plan[1 + (spot >> 7), spot & (LANES - 1)]

    def block_of(g):
        return pl.ds(pl.multiple_of((jnp.maximum(code_at(g * GROUP), 0) >> 24) * TILE, TILE), TILE)

    def make_ratio(g, i):
        rows = users[block_of(g), :]
        codes = [code_at(g * GROUP + j) for j in range(GROUP)]
        slots = [jnp.maximum(code, 0) for code in codes]
        for j, slot in enumerate(slots):
            item = pl.multiple_of(((slot >> 8) & 255) * TILE, TILE)
            scale = day_rows[pl.ds(slot & 255, 1), :].astype(jnp.bfloat16)
            weighted[i][j * TILE : (j + 1) * TILE, :] = items[pl.ds(item, TILE), :] * scale
            model = jnp.dot(
                rows * scale, across[:, pl.ds(item, TILE)], preferred_element_type=jnp.float32
            )
            ratio = counts[(slot >> 16) & 255].astype(jnp.float32) / model
            ratios[i][:, j * TILE : (j + 1) * TILE] = jnp.where(codes[j] >= 0, ratio, 0.0).astype(
                jnp.bfloat16
            )

    def add_terms(g, i):
        phi[block_of(g), :] += jnp.dot(
            ratios[i][...], weighted[i][...], preferred_element_type=jnp.float32
        )

    def turn(t, ready):
        need = jnp.maximum(plan[0, NEEDS + t], ready)
        lax.fori_loop(ready, need, wait_part, 0)
        for i in range(UNROLL):
            g = t * UNROLL + i
            make_ratio(g, i)
            add_terms(jnp.maximum(g - 1, 0), (i - 1) % UNROLL)
        return need

    turns = (groups + UNROLL - 1 - TAIL) // UNROLL
    ready = lax.fori_loop(0, turns, turn, jnp.int32(FIRST))
    lax.fori_loop(ready, all_parts, wait_part, 0)
    first = turns * UNROLL
    rest = groups - first

    def tail(count):
        for i in range(count):
            make_ratio(first + i, i)
            add_terms(jnp.maximum(first + i - 1, 0), (i - 1) % UNROLL)
        add_terms(jnp.maximum(first + count - 1, 0), (count - 1) % UNROLL)

    for count in range(TAIL + 1):
        chosen = rest <= 0 if count == 0 else rest == count
        pl.when(chosen)(functools.partial(tail, count))

    own = kept.shape[1]
    core = lax.axis_index("day") & 1
    for j in range(kept.shape[0]):
        kept[j] = phi[pl.ds(pl.multiple_of((2 * j + core) * own, own), own), :]
        sent[j] = phi[pl.ds(pl.multiple_of((2 * j + 1 - core) * own, own), own), :]


def finish_kernel(n_item, chips, received, user_factors, out):
    rank = user_factors.shape[1]
    phi = jnp.sum(received[:, :, 0:rank].astype(jnp.float32), axis=0)
    for q in range(rank // LANES):
        cols = slice(q * LANES, (q + 1) * LANES)
        item = received[q % chips, :, rank:].astype(jnp.float32)
        for i in range(1, n_item):
            item = item + received[i * chips + q % chips, :, rank:].astype(jnp.float32)
        day = received[q * chips, :, rank:].astype(jnp.float32)
        for k in range(1, chips):
            day = day + received[q * chips + k, :, rank:].astype(jnp.float32)
        at = 2 * (q // chips)
        totals = (item[at : at + 1] + item[at + 1 : at + 2]) * (
            day[DAY_ROW : DAY_ROW + 1] + day[DAY_ROW + 1 : DAY_ROW + 2]
        )
        out[:, cols] = user_factors[:, cols] * phi[:, cols] / totals


def solution(mesh):
    n_item, n_day = mesh.shape["item"], mesh.shape["day"]
    devices = n_item * n_day
    axes = ("item", "day")
    mates = [(k, k ^ 1) for k in range(n_day)]

    def per_device(user_factors, item_factors, day_factors, tile_counts, tile_index, tile_live):
        own, rank = user_factors.shape
        blocks = own * devices // TILE
        cap = tile_counts.shape[0]
        day_space = round_up(day_factors.shape[0], 8)
        groups = round_up(cap // GROUP + blocks, UNROLL)
        plan_shape = (1 + pl.cdiv(groups * GROUP, LANES), LANES)
        mate_counts, mate_index, mate_live, mate_days = (
            lax.ppermute(x, "day", mates)
            for x in (tile_counts, tile_index, tile_live, day_factors)
        )
        spread = jnp.broadcast_to(user_factors.astype(jnp.bfloat16)[None], (devices, own, rank))
        gathered = lax.all_to_all(spread, axes, 0, 0, tiled=True).reshape(devices * own, rank)
        plan, items, across, day_rows, first_counts = pl.pallas_call(
            functools.partial(plan_kernel, blocks),
            out_shape=(
                jax.ShapeDtypeStruct(plan_shape, jnp.int32),
                jax.ShapeDtypeStruct(item_factors.shape, jnp.bfloat16),
                jax.ShapeDtypeStruct(item_factors.shape[::-1], jnp.bfloat16),
                jax.ShapeDtypeStruct((2 * day_space, rank), jnp.float32),
                jax.ShapeDtypeStruct((FIRST * CHUNK, *tile_counts.shape[1:]), jnp.bfloat16),
            ),
            in_specs=[SMEM, SMEM, VMEM, VMEM, VMEM, HBM, HBM, HBM],
            out_specs=(VMEM, VMEM, VMEM, VMEM, VMEM),
            scratch_shapes=[
                pltpu.VMEM(day_factors.shape, jnp.bfloat16),
                pltpu.SemaphoreType.DMA((3,)),
            ],
            compiler_params=pltpu.CompilerParams(vmem_limit_bytes=PLAN_MIB * MIB),
        )(
            tile_live, mate_live, tile_index, mate_index, mate_days,
            day_factors, item_factors, tile_counts,
        )
        kept, sent = pl.pallas_call(
            tiles_kernel,
            out_shape=(jax.ShapeDtypeStruct((devices // 2, own, rank), jnp.float32),) * 2,
            in_specs=[HBM, HBM, HBM, VMEM, VMEM, VMEM, VMEM, VMEM],
            out_specs=(VMEM, VMEM),
            scratch_shapes=[
                pltpu.SMEM(plan_shape, jnp.int32),
                pltpu.VMEM((cap + 2 * CHUNK, *tile_counts.shape[1:]), jnp.bfloat16),
                pltpu.VMEM((blocks * TILE, rank), jnp.float32),
                pltpu.SemaphoreType.DMA,
                pltpu.SemaphoreType.DMA((cap // CHUNK + 2,)),
            ]
            + [pltpu.VMEM((GROUP * TILE, rank), jnp.bfloat16)] * UNROLL
            + [pltpu.VMEM((TILE, GROUP * TILE), jnp.bfloat16)] * UNROLL,
            compiler_params=pltpu.CompilerParams(vmem_limit_bytes=50 * MIB),
        )(plan, tile_counts, mate_counts, first_counts, gathered, items, across, day_rows)
        chip_sum = (kept + lax.ppermute(sent, "day", mates)).astype(jnp.bfloat16)
        extra = pl.pallas_call(
            functools.partial(sums_kernel, n_day // 2),
            out_shape=jax.ShapeDtypeStruct((8, LANES), jnp.bfloat16),
            in_specs=[ANY, VMEM, VMEM],
            out_specs=VMEM,
            compiler_params=pltpu.CompilerParams(vmem_limit_bytes=16 * MIB),
        )(kept, items, day_rows)
        sums = jnp.broadcast_to(extra[None], (devices // 2, 8, LANES))
        received = lax.all_to_all(
            jnp.concatenate([chip_sum, sums], axis=2),
            axes,
            0,
            0,
            axis_index_groups=[list(range(c, devices, 2)) for c in range(2)],
            tiled=True,
        )
        return pl.pallas_call(
            functools.partial(finish_kernel, n_item, n_day // 2),
            out_shape=jax.ShapeDtypeStruct((own, rank), jnp.float32),
            in_specs=[VMEM, VMEM],
            out_specs=VMEM,
            compiler_params=pltpu.CompilerParams(vmem_limit_bytes=16 * MIB),
        )(received, user_factors)

    in_specs = (
        P(axes, None),
        P("item", None),
        P("day", None),
        P(axes, None, None),
        P(None, axes),
        P(axes),
    )
    return jax.shard_map(
        per_device, mesh=mesh, in_specs=in_specs, out_specs=P(axes, None), check_vma=False
    )
```
